256 devices in a mesh: blk: 64 (over x_lo, z, y), head: 4 (over x_hi, core).
Axes of the slice: x: 4 (x_hi: 2, x_lo: 2; x = x_hi * 2 + x_lo), y: 4, z: 8, core: 2. Of those that a mesh axis runs over, the one named last changes fastest.
Arguments:
- queries: bfloat16 [8192, 1536], P('blk', 'head'), may hold values from -5 to 5
- keys: bfloat16 [8192, 1536], P('blk', 'head'), may hold values from -5 to 5
- values: bfloat16 [8192, 1536], P('blk', 'head'), may hold values from -6 to 6
- tan_queries: bfloat16 [8192, 1536], P('blk', 'head'), may hold values from -6 to 6
- tan_keys: bfloat16 [8192, 1536], P('blk', 'head'), may hold values from -6 to 6
- tan_values: bfloat16 [8192, 1536], P('blk', 'head'), may hold values from -6 to 6
- out_weight: bfloat16 [1536, 3072], P('head'), may hold values from -0.625 to 0.625
Outputs:
- attended: bfloat16 [8192, 3072], P(('blk', 'head'))
- tan_attended: bfloat16 [8192, 3072], P(('blk', 'head'))
The draws below stay inside these ranges and needn't reach their ends.
All inputs are finite; a program needn't handle non-finite values.
Results may differ from the reference program's by a relative error of at most 0.013.
Values may be sent and summed in bfloat16 or wider, within the bound.
No kernel may reach another device: no remote copies, remote signals or barrier semaphores. Data moves between devices by JAX's collectives and lax.ppermute only.
A program may use at most 128 MiB of HBM per device.

```python
import math
import jax
import jax.numpy as jnp
from jax import lax

D = 3072
HEADS = 12
HEAD_DIM = 128
TOKENS = 8192


def draw_queries(key, part):
    key = jax.random.fold_in(key, 1)
    drawn = jnp.clip(1.6 * jax.random.normal(key, (TOKENS, HEADS, HEAD_DIM), jnp.float32), -5.0, 5.0)
    return drawn.reshape(TOKENS, HEADS * HEAD_DIM).astype(jnp.bfloat16)


def draw_keys(key, part):
    key = jax.random.fold_in(key, 2)
    drawn = jnp.clip(1.6 * jax.random.normal(key, (TOKENS, HEADS, HEAD_DIM), jnp.float32), -5.0, 5.0)
    return drawn.reshape(TOKENS, HEADS * HEAD_DIM).astype(jnp.bfloat16)


def block_levels(key, dims, shards, low, largest):
    def one(axis_at, blocks):
        steps = jax.random.uniform(jax.random.fold_in(jax.random.fold_in(key, 6), axis_at), (blocks,), jnp.float32, low / len(shards), largest / len(shards))
        return jnp.repeat(jnp.exp(steps), dims[axis_at] // blocks).reshape((-1,) + (1,) * (len(dims) - axis_at - 1))

    factor_of = one(*shards[0])
    for cut in shards[1:]:
        factor_of = factor_of * one(*cut)
    return factor_of


def normal_values(stream_key, shape, deviation, reach, cuts=(), held_as=jnp.bfloat16):
    values = deviation * jax.random.normal(stream_key, shape, jnp.float32)
    if cuts:
        values = values * block_levels(stream_key, shape, cuts, -0.22, 0.18)
    return jnp.clip(values, -reach, reach).astype(held_as)


def setup_inputs(seed: int = 0) -> dict:
    streams_of = jax.random.split(jax.random.key(seed), 8)
    queries = draw_queries(jax.random.fold_in(streams_of[7], 71), 0)
    keys = draw_keys(jax.random.fold_in(streams_of[7], 71), 0)
    values = normal_values(streams_of[2], (TOKENS, HEADS * HEAD_DIM), 1.0, 6.0, ((0, 64), (1, 4)))
    tan_queries = normal_values(streams_of[3], (TOKENS, HEADS * HEAD_DIM), 1.0, 6.0, ((0, 64), (1, 4)))
    tan_keys = normal_values(streams_of[4], (TOKENS, HEADS * HEAD_DIM), 1.0, 6.0, ((0, 64), (1, 4)))
    tan_values = normal_values(streams_of[5], (TOKENS, HEADS * HEAD_DIM), 1.0, 6.0, ((0, 64), (1, 4)))
    out_weight = normal_values(streams_of[6], (HEADS * HEAD_DIM, D), (HEADS * HEAD_DIM // 16) ** -0.5, 0.625, ((0, 4),))
    return {"queries": queries, "keys": keys, "values": values, "tan_queries": tan_queries, "tan_keys": tan_keys, "tan_values": tan_values, "out_weight": out_weight}


def head_block(query_block, tan_query_block, head_keys, head_values, head_tan_keys, head_tan_values, score_scale):
    scores = jnp.dot(query_block, head_keys.T, preferred_element_type=jnp.float32) * score_scale
    tan_scores = (jnp.dot(tan_query_block, head_keys.T, preferred_element_type=jnp.float32) + jnp.dot(query_block, head_tan_keys.T, preferred_element_type=jnp.float32)) * score_scale
    row_max = lax.optimization_barrier(jnp.max(scores, axis=1, keepdims=True))
    weights = jnp.exp(scores - row_max)
    tangent_weights = weights * tan_scores
    denom = lax.optimization_barrier(jnp.sum(weights, axis=1, keepdims=True))
    tan_denom = lax.optimization_barrier(jnp.sum(tangent_weights, axis=1, keepdims=True))
    weights_low = weights.astype(jnp.bfloat16)
    tangent_low = tangent_weights.astype(jnp.bfloat16)
    accum = jnp.dot(weights_low, head_values, preferred_element_type=jnp.float32)
    tan_accum = jnp.dot(tangent_low, head_values, preferred_element_type=jnp.float32) + jnp.dot(weights_low, head_tan_values, preferred_element_type=jnp.float32)
    head_out = accum / denom
    head_tan = tan_accum / denom - head_out * (tan_denom / denom)
    return (head_out.astype(jnp.bfloat16), head_tan.astype(jnp.bfloat16))

def reference(queries, keys, values, tan_queries, tan_keys, tan_values, out_weight):
    score_scale = 1.0 / math.sqrt(HEAD_DIM)
    block_span = math.gcd(TOKENS, 1024)

    def per_head(head_index):
        first_column = head_index * HEAD_DIM

        def head_columns(matrix):
            return lax.dynamic_slice_in_dim(matrix, first_column, HEAD_DIM, 1)
        head_queries = head_columns(queries)
        head_tan_queries = head_columns(tan_queries)
        head_keys = head_columns(keys)
        head_values = head_columns(values)
        head_tan_keys = head_columns(tan_keys)
        head_tan_values = head_columns(tan_values)

        def per_block(block_index):
            first_row = block_index * block_span
            return head_block(lax.dynamic_slice_in_dim(head_queries, first_row, block_span, 0), lax.dynamic_slice_in_dim(head_tan_queries, first_row, block_span, 0), head_keys, head_values, head_tan_keys, head_tan_values, score_scale)
        head_out, head_tan = lax.map(per_block, jnp.arange(TOKENS // block_span, dtype=jnp.int32))
        return (head_out.reshape(TOKENS, HEAD_DIM), head_tan.reshape(TOKENS, HEAD_DIM))
    out_heads, tan_heads = lax.map(per_head, jnp.arange(HEADS, dtype=jnp.int32))
    out_rows = out_heads.transpose(1, 0, 2).reshape(TOKENS, HEADS * HEAD_DIM)
    tan_rows = tan_heads.transpose(1, 0, 2).reshape(TOKENS, HEADS * HEAD_DIM)
    attended = jnp.dot(out_rows, out_weight, preferred_element_type=jnp.float32).astype(jnp.bfloat16)
    tan_attended = jnp.dot(tan_rows, out_weight, preferred_element_type=jnp.float32).astype(jnp.bfloat16)
    return (attended, tan_attended)
```

```python
import functools
import math

import jax
import jax.numpy as jnp
from jax import lax
from jax.experimental import pallas as pl
from jax.experimental.pallas import tpu as pltpu
from jax.sharding import Mesh, PartitionSpec as P

DH = 128
NH = 3
TB = 128
SCALE = 1.0 / math.sqrt(DH)
SCALE2 = SCALE * math.log2(math.e)
SIZES = {"xlo": 2, "z": 8, "y": 4, "xhi": 2, "core": 2}
AXES = ("xlo", "z", "y", "xhi", "core")
PART = 2 * NH * 32 + 16
F32, BF16 = jnp.float32, jnp.bfloat16
VMEM = pl.BlockSpec(memory_space=pltpu.VMEM)
SMEM = pl.BlockSpec(memory_space=pltpu.SMEM)


def shift(x, axis, by):
    n = SIZES[axis]
    return lax.ppermute(x, axis, [(i, (i + by) % n) for i in range(n)])


def mm(a, b):
    return jnp.dot(a, b, preferred_element_type=F32)


def pack_kernel(q, k, v, tq, tk, tv, kp, qp):
    for h in range(NH):
        cols = slice(h * DH, (h + 1) * DH)
        kp[2 * h] = k[:, cols]
        kp[2 * h + 1] = tk[:, cols]
        kp[2 * NH + 2 * h] = v[:, cols].T
        kp[2 * NH + 2 * h + 1] = tv[:, cols].T
        qp[2 * h] = q[:, cols].T
        qp[2 * h + 1] = tq[:, cols].T


def pack(q, k, v, tq, tk, tv):
    return pl.pallas_call(
        pack_kernel,
        out_shape=(
            jax.ShapeDtypeStruct((4 * NH, TB, DH), BF16),
            jax.ShapeDtypeStruct((2 * NH, DH, TB), BF16),
        ),
        in_specs=[VMEM] * 6,
        out_specs=(VMEM, VMEM),
        name="pack",
    )(q, k, v, tq, tk, tv)


def unit(qs, ks, vs, s, h):
    q = jnp.concatenate([qs[s][0, 2 * h], qs[s][1, 2 * h]], axis=1)
    tq = jnp.concatenate([qs[s][0, 2 * h + 1], qs[s][1, 2 * h + 1]], axis=1)
    k = jnp.concatenate([r[2 * h] for r in ks], axis=0)
    tk = jnp.concatenate([r[2 * h + 1] for r in ks], axis=0)
    scores = mm(k, q)
    tan = mm(jnp.concatenate([k, tk], axis=1), jnp.concatenate([tq, q], axis=0))
    return scores, tan


def attend_kernel(nk, first, last, *refs):
    refs = list(refs)
    pos = refs.pop(0) if last else None
    qs = [refs.pop(0) for _ in range(4)]
    if nk == 0:
        kparts, vparts, vbase = [refs.pop(0)], [refs.pop(0)], 0
    else:
        kparts = [refs.pop(0) for _ in range(nk)]
        vparts, vbase = kparts, 2 * NH
    if not first:
        acc_in, st_in = refs.pop(0), refs.pop(0)
    if last:
        (out,) = refs
    else:
        acc_out, st_out = refs
    for s in range(4):
        stat_rows = [[], []]
        for h in range(NH):
            scores, tan = unit(qs, kparts, vparts, s, h)
            top = jnp.max(scores, axis=0, keepdims=True) * SCALE2
            if not first:
                st = st_in[s, h]
                old = st[0:1]
                top = jnp.maximum(old, top)
                keep = jnp.exp2(old - top)
            w = jnp.exp2(scores * SCALE2 - top)
            tw = w * tan
            den = jnp.sum(w, axis=0, keepdims=True)
            tden = jnp.sum(tw, axis=0, keepdims=True)
            wl, twl = w.astype(BF16), tw.astype(BF16)
            v = jnp.concatenate([r[vbase + 2 * h] for r in vparts], axis=1)
            tv = jnp.concatenate([r[vbase + 2 * h + 1] for r in vparts], axis=1)
            both = mm(jnp.concatenate([v, tv], axis=0), wl)
            a = both[:DH]
            b = both[DH:] + mm(v, twl) * SCALE
            if not first:
                a = a + acc_in[s, h, :DH] * keep
                b = b + acc_in[s, h, DH:] * keep
                den = den + st[1:2] * keep
                tden = tden + st[2:3] * keep
            if not last:
                acc_out[s, h, :DH] = a
                acc_out[s, h, DH:] = b
                st_out[s, h] = jnp.concatenate([top, den, tden, jnp.zeros((5, 2 * TB), F32)], axis=0)
                continue
            inv = 1.0 / den
            ratio = tden * SCALE * inv
            o = a * inv
            t = b * inv - o * ratio
            lse = top + jnp.log2(den)
            l0 = lse.astype(BF16)
            rest = lse - l0.astype(F32)
            l1 = rest.astype(BF16)
            l2 = (rest - l1.astype(F32)).astype(BF16)
            r0 = ratio.astype(BF16)
            r1 = (ratio - r0.astype(F32)).astype(BF16)
            for x in range(2):
                lanes = slice(x * TB, (x + 1) * TB)
                place = pos[2 * s + x]
                ot = o[:, lanes].T.astype(BF16)
                tt = t[:, lanes].T.astype(BF16)
                for to in range(4):
                    rows = slice(to * 32, (to + 1) * 32)
                    out[place, to, 64 * h : 64 * h + 32] = ot[rows]
                    out[place, to, 64 * h + 32 : 64 * h + 64] = tt[rows]
                stat_rows[x] += [piece[:, lanes].astype(F32) for piece in (l0, l1, l2, r0, r1)]
        if last:
            for x in range(2):
                rows = jnp.concatenate(stat_rows[x] + [jnp.zeros((1, TB), F32)], axis=0).astype(BF16)
                for to in range(4):
                    out[pos[2 * s + x], to, 64 * NH : PART] = rows


def attend(qs, blocks, state=None, pos=None):
    halves = blocks[0].shape[0] == 2 * NH
    first, last = state is None, pos is not None
    nk = 0 if halves else len(blocks)
    keys = TB * max(nk, 1)
    operands = ([pos] if last else []) + list(qs) + list(blocks) + ([] if first else list(state))
    specs = ([SMEM] if last else []) + [VMEM] * (len(operands) - last)
    if last:
        out_shape = jax.ShapeDtypeStruct((8, 4, PART, DH), BF16)
        out_specs = VMEM
    else:
        out_shape = (
            jax.ShapeDtypeStruct((4, NH, 2 * DH, 2 * TB), F32),
            jax.ShapeDtypeStruct((4, NH, 8, 2 * TB), F32),
        )
        out_specs = (VMEM, VMEM)
    n = len(operands)
    alias = {} if first or last else {n - 2: 0, n - 1: 1}
    return pl.pallas_call(
        functools.partial(attend_kernel, nk, first, last),
        out_shape=out_shape,
        in_specs=specs,
        out_specs=out_specs,
        input_output_aliases=alias,
        compiler_params=pltpu.CompilerParams(vmem_limit_bytes=32 << 20),
        cost_estimate=pl.CostEstimate(
            flops=2 * 8 * TB * DH * NH * keys * 8, bytes_accessed=8 << 20, transcendentals=8 * TB * NH * keys
        ),
        name=f"attend{keys}",
    )(*operands)


def project_kernel(me, got, w0, w1, w2, w3, out, tan_out, cols, rows):
    @pl.when(pl.program_id(0) == 0)
    def _():
        share, tilt = [], []
        for g in range(4):
            st = got[:, lax.bitwise_xor(me[0], g), 64 * NH : PART].astype(F32)
            for h in range(NH):
                lse = st[:, 5 * h] + st[:, 5 * h + 1] + st[:, 5 * h + 2]
                ratio = st[:, 5 * h + 3] + st[:, 5 * h + 4]
                w = jnp.exp2(lse - jnp.max(lse, axis=0, keepdims=True))
                w = w / jnp.sum(w, axis=0, keepdims=True)
                share.append(w)
                tilt.append(w * (ratio - jnp.sum(w * ratio, axis=0, keepdims=True)))
        pad = jnp.zeros((32, TB), F32)
        cols[:, :128] = jnp.concatenate(share + [pad], axis=0).T
        cols[:, 128:] = jnp.concatenate(tilt + [pad], axis=0).T
        mine = cols[pl.ds(pl.multiple_of(me[0] * 32, 32), 32)]
        for g in range(4):
            j = lax.bitwise_xor(me[0], g)
            for h in range(NH):
                o = t = None
                for i in range(8):
                    c = (g * NH + h) * 8 + i
                    oi = got[i, j, 64 * h : 64 * h + 32].astype(F32)
                    ti = got[i, j, 64 * h + 32 : 64 * h + 64].astype(F32)
                    a, b = mine[:, c : c + 1], mine[:, 128 + c : 129 + c]
                    o = oi * a if o is None else o + oi * a
                    t = ti * a + oi * b if t is None else t + (ti * a + oi * b)
                rows[g, :32, h * DH : (h + 1) * DH] = o.astype(BF16)
                rows[g, 32:, h * DH : (h + 1) * DH] = t.astype(BF16)

    total = mm(rows[0], w0[...]) + mm(rows[1], w1[...]) + mm(rows[2], w2[...]) + mm(rows[3], w3[...])
    out[...] = total[:32].astype(BF16)
    tan_out[...] = total[32:].astype(BF16)


def project(me, got, weights):
    depth, width = weights[0].shape
    step = 512
    wspec = pl.BlockSpec((depth, step), lambda i: (0, i))
    ospec = pl.BlockSpec((32, step), lambda i: (0, i))
    oshape = jax.ShapeDtypeStruct((32, width), BF16)
    return pl.pallas_call(
        project_kernel,
        out_shape=(oshape, oshape),
        grid=(width // step,),
        in_specs=[SMEM, pl.BlockSpec((8, 4, PART, DH), lambda i: (0, 0, 0, 0))] + [wspec] * 4,
        out_specs=(ospec, ospec),
        scratch_shapes=[pltpu.VMEM((TB, 256), F32), pltpu.VMEM((4, 64, NH * DH), BF16)],
        compiler_params=pltpu.CompilerParams(vmem_limit_bytes=32 << 20),
        cost_estimate=pl.CostEstimate(
            flops=2 * 64 * 4 * depth * width, bytes_accessed=4 * depth * width * 2, transcendentals=0
        ),
        name="project",
    )(me, got, *weights)


def on_device(queries, keys, values, tan_queries, tan_keys, tan_values, out_weight):
    xlo, y = lax.axis_index("xlo"), lax.axis_index("y")
    me = lax.axis_index("xhi") * 2 + lax.axis_index("core")
    kp, qp = pack(queries, keys, values, tan_queries, tan_keys, tan_values)

    right, left = [kp], [kp]
    for _ in range(3):
        right.append(shift(right[-1], "z", 1))
        left.append(shift(left[-1], "z", -1))
    far = (shift(right[-1][: 2 * NH], "z", 1), shift(left[-1][2 * NH :], "z", -1))

    q0 = jnp.stack([qp, shift(qp, "xlo", 1)])
    qs = (q0, shift(q0, "y", 1), shift(q0, "y", -1), shift(q0, "y", 2))
    pos = jnp.stack([(xlo ^ x) * 4 + (y + d) % 4 for d in (0, 3, 1, 2) for x in (0, 1)]).astype(jnp.int32)

    across = lax.ppermute(out_weight, ("xlo", "xhi"), [(2, 1), (1, 2), (3, 0), (0, 3)])
    weights = (out_weight, shift(out_weight, "core", 1), across, shift(across, "core", 1))

    state = attend(qs, (kp, right[1], left[1]))
    state = attend(qs, (right[2], left[2]), state)
    state = attend(qs, (right[3], left[3]), state)
    sent = attend(qs, far, state, pos)
    got = lax.all_to_all(sent.reshape(32, PART, DH), ("xlo", "y", "xhi", "core"), 0, 0, tiled=True)
    return project(jnp.reshape(me, (1,)).astype(jnp.int32), got.reshape(8, 4, PART, DH), weights)


def solution(mesh):
    fine = Mesh(mesh.devices.reshape([SIZES[a] for a in AXES]), AXES)
    blk, head = ("xlo", "z", "y"), ("xhi", "core")
    spec = P(blk, head)
    return jax.shard_map(
        on_device,
        mesh=fine,
        in_specs=(spec,) * 6 + (P(head, None),),
        out_specs=(P(blk + head, None),) * 2,
        check_vma=False,
    )
```

```python
import functools
import math

import jax
import jax.numpy as jnp
from jax import lax
from jax.experimental import pallas as pl
from jax.experimental.pallas import tpu as pltpu
from jax.sharding import Mesh, PartitionSpec as P

DH = 128
NH = 3
TB = 128
SCALE = 1.0 / math.sqrt(DH)
SCALE2 = SCALE * math.log2(math.e)
SIZES = {"xlo": 2, "z": 8, "y": 4, "xhi": 2, "core": 2}
AXES = ("xlo", "z", "y", "xhi", "core")
PART = 2 * NH * 32 + 16
F32, BF16 = jnp.float32, jnp.bfloat16
VMEM = pl.BlockSpec(memory_space=pltpu.VMEM)
SMEM = pl.BlockSpec(memory_space=pltpu.SMEM)


def shift(x, axis, by):
    n = SIZES[axis]
    return lax.ppermute(x, axis, [(i, (i + by) % n) for i in range(n)])


def mm(a, b):
    return jnp.dot(a, b, preferred_element_type=F32)


def pack_kernel(q, k, v, tq, tk, tv, kp, qp):
    for h in range(NH):
        cols = slice(h * DH, (h + 1) * DH)
        kp[2 * h] = k[:, cols]
        kp[2 * h + 1] = tk[:, cols]
        kp[2 * NH + 2 * h] = v[:, cols].T
        kp[2 * NH + 2 * h + 1] = tv[:, cols].T
        qp[2 * h] = q[:, cols].T
        qp[2 * h + 1] = tq[:, cols].T


def pack(q, k, v, tq, tk, tv):
    return pl.pallas_call(
        pack_kernel,
        out_shape=(
            jax.ShapeDtypeStruct((4 * NH, TB, DH), BF16),
            jax.ShapeDtypeStruct((2 * NH, DH, TB), BF16),
        ),
        in_specs=[VMEM] * 6,
        out_specs=(VMEM, VMEM),
        name="pack",
    )(q, k, v, tq, tk, tv)


def unit(qs, ks, vs, s, h):
    q = jnp.concatenate([qs[s][0, 2 * h], qs[s][1, 2 * h]], axis=1)
    tq = jnp.concatenate([qs[s][0, 2 * h + 1], qs[s][1, 2 * h + 1]], axis=1)
    k = jnp.concatenate([r[2 * h] for r in ks], axis=0)
    tk = jnp.concatenate([r[2 * h + 1] for r in ks], axis=0)
    scores = mm(k, q)
    tan = mm(jnp.concatenate([k, tk], axis=1), jnp.concatenate([tq, q], axis=0))
    return scores, tan


def attend_kernel(nk, first, last, *refs):
    refs = list(refs)
    at = refs.pop(0) if last else None
    qs = [refs.pop(0) for _ in range(4)]
    if nk == 0:
        kparts, vparts, vbase = [refs.pop(0)], [refs.pop(0)], 0
    else:
        kparts = [refs.pop(0) for _ in range(nk)]
        vparts, vbase = kparts, 2 * NH
    if not first:
        acc_in, st_in = refs.pop(0), refs.pop(0)
    if last:
        (out,) = refs
    else:
        acc_out, st_out = refs
    stat_rows = {}

    def block(s, x):
        return lax.bitwise_xor(at[0], x) * 4 + lax.bitwise_and(at[1] + (0, 3, 1, 2)[s], 3)

    def finish(s, h, scores, tan):
        top = jnp.max(scores, axis=0, keepdims=True) * SCALE2
        if not first:
            st = st_in[s, h]
            old = st[0:1]
            top = jnp.maximum(old, top)
            keep = jnp.exp2(old - top)
        w = jnp.exp2(scores * SCALE2 - top)
        tw = w * tan
        den = jnp.sum(w, axis=0, keepdims=True)
        tden = jnp.sum(tw, axis=0, keepdims=True)
        wl, twl = w.astype(BF16), tw.astype(BF16)
        v = jnp.concatenate([r[vbase + 2 * h] for r in vparts], axis=1)
        tv = jnp.concatenate([r[vbase + 2 * h + 1] for r in vparts], axis=1)
        both = mm(jnp.concatenate([v, tv], axis=0), wl)
        a = both[:DH]
        b = both[DH:] + mm(v, twl) * SCALE
        if not first:
            a = a + acc_in[s, h, :DH] * keep
            b = b + acc_in[s, h, DH:] * keep
            den = den + st[1:2] * keep
            tden = tden + st[2:3] * keep
        if not last:
            acc_out[s, h, :DH] = a
            acc_out[s, h, DH:] = b
            st_out[s, h] = jnp.concatenate([top, den, tden, jnp.zeros((5, 2 * TB), F32)], axis=0)
            return
        inv = 1.0 / den
        ratio = tden * SCALE * inv
        o = a * inv
        t = b * inv - o * ratio
        lse = top + jnp.log2(den)
        l0 = lse.astype(BF16)
        rest = lse - l0.astype(F32)
        l1 = rest.astype(BF16)
        l2 = (rest - l1.astype(F32)).astype(BF16)
        r0 = ratio.astype(BF16)
        r1 = (ratio - r0.astype(F32)).astype(BF16)
        for x in range(2):
            lanes = slice(x * TB, (x + 1) * TB)
            ot = o[:, lanes].astype(BF16).T
            tt = t[:, lanes].astype(BF16).T
            for to in range(4):
                rows = slice(to * 32, (to + 1) * 32)
                out[block(s, x), to, 64 * h : 64 * h + 32] = ot[rows]
                out[block(s, x), to, 64 * h + 32 : 64 * h + 64] = tt[rows]
            stat_rows.setdefault((s, x), []).extend(
                piece[:, lanes].astype(F32) for piece in (l0, l1, l2, r0, r1)
            )
        if h == NH - 1:
            for x in range(2):
                rows = jnp.concatenate(stat_rows[s, x] + [jnp.zeros((1, TB), F32)], axis=0).astype(BF16)
                for to in range(4):
                    out[block(s, x), to, 64 * NH : PART] = rows

    waiting = []
    for s in range(4):
        for h in range(NH):
            waiting.append((s, h, *unit(qs, kparts, vparts, s, h)))
            if len(waiting) > 2:
                finish(*waiting.pop(0))
    for item in waiting:
        finish(*item)


def attend(qs, blocks, state=None, at=None):
    halves = blocks[0].shape[0] == 2 * NH
    first, last = state is None, at is not None
    nk = 0 if halves else len(blocks)
    keys = TB * max(nk, 1)
    operands = ([at] if last else []) + list(qs) + list(blocks) + ([] if first else list(state))
    specs = ([SMEM] if last else []) + [VMEM] * (len(operands) - last)
    if last:
        out_shape = jax.ShapeDtypeStruct((8, 4, PART, DH), BF16)
        out_specs = VMEM
    else:
        out_shape = (
            jax.ShapeDtypeStruct((4, NH, 2 * DH, 2 * TB), F32),
            jax.ShapeDtypeStruct((4, NH, 8, 2 * TB), F32),
        )
        out_specs = (VMEM, VMEM)
    n = len(operands)
    alias = {} if first or last else {n - 2: 0, n - 1: 1}
    return pl.pallas_call(
        functools.partial(attend_kernel, nk, first, last),
        out_shape=out_shape,
        in_specs=specs,
        out_specs=out_specs,
        input_output_aliases=alias,
        compiler_params=pltpu.CompilerParams(vmem_limit_bytes=32 << 20),
        cost_estimate=pl.CostEstimate(
            flops=2 * 8 * TB * DH * NH * keys * 8, bytes_accessed=8 << 20, transcendentals=8 * TB * NH * keys
        ),
        name=f"attend{keys}",
    )(*operands)


def project_kernel(me, got, w0, w1, w2, w3, out, tan_out, rows):
    share, tilt = [], []
    for g in range(4):
        st = got[:, lax.bitwise_xor(me[0], g), 64 * NH : PART].astype(F32)
        for h in range(NH):
            lse = st[:, 5 * h] + st[:, 5 * h + 1] + st[:, 5 * h + 2]
            ratio = st[:, 5 * h + 3] + st[:, 5 * h + 4]
            w = jnp.exp2(lse - jnp.max(lse, axis=0, keepdims=True))
            w = w / jnp.sum(w, axis=0, keepdims=True)
            share.append(w)
            tilt.append(w * (ratio - jnp.sum(w * ratio, axis=0, keepdims=True)))
    group = lax.broadcasted_iota(jnp.int32, (8, TB), 1) // 32
    part = lax.broadcasted_iota(jnp.int32, (8, TB), 0) % 4
    row = lax.broadcasted_iota(jnp.int32, (32, TB), 0)
    diagonal = lax.broadcasted_iota(jnp.int32, (32, TB), 1) % 32 == row

    def spread(w):
        turned = w
        for i in range(1, 4):
            turned = jnp.where(part == i, pltpu.roll(w, 32 * i, axis=1), turned)
        turned = pltpu.roll(turned, lax.rem(4 - me[0], 4) * 32, axis=1)
        picked = jnp.where(group == part, turned, 0.0)
        halves = [jnp.sum(picked[4 * i : 4 * i + 4], axis=0, keepdims=True) for i in range(2)]
        return jnp.concatenate([jnp.where(diagonal, half, 0.0) for half in halves], axis=1).astype(BF16)

    for g in range(4):
        j = lax.bitwise_xor(me[0], g)
        for h in range(NH):
            mix = jnp.concatenate([spread(share[g * NH + h]), spread(tilt[g * NH + h])], axis=0)
            o = jnp.concatenate([got[i, j, 64 * h : 64 * h + 32] for i in range(8)], axis=0)
            t = jnp.concatenate([got[i, j, 64 * h + 32 : 64 * h + 64] for i in range(8)], axis=0)
            both = mm(mix, jnp.concatenate([o, t], axis=1))
            rows[g, :32, h * DH : (h + 1) * DH] = both[:32, :DH].astype(BF16)
            rows[g, 32:, h * DH : (h + 1) * DH] = (both[:32, DH:] + both[32:, :DH]).astype(BF16)

    width = out.shape[1]
    for c in range(0, width, 512):
        cols = slice(c, c + 512)
        total = mm(rows[0], w0[:, cols]) + mm(rows[1], w1[:, cols])
        total = total + mm(rows[2], w2[:, cols]) + mm(rows[3], w3[:, cols])
        out[:, cols] = total[:32].astype(BF16)
        tan_out[:, cols] = total[32:].astype(BF16)


def project(me, got, weights):
    depth, width = weights[0].shape
    oshape = jax.ShapeDtypeStruct((32, width), BF16)
    return pl.pallas_call(
        project_kernel,
        out_shape=(oshape, oshape),
        in_specs=[SMEM] + [VMEM] * 5,
        out_specs=(VMEM, VMEM),
        scratch_shapes=[pltpu.VMEM((4, 64, NH * DH), BF16)],
        compiler_params=pltpu.CompilerParams(vmem_limit_bytes=32 << 20),
        cost_estimate=pl.CostEstimate(
            flops=2 * 64 * 4 * depth * width, bytes_accessed=4 * depth * width * 2, transcendentals=0
        ),
        name="project",
    )(me, got, *weights)


def on_device(queries, keys, values, tan_queries, tan_keys, tan_values, out_weight):
    xlo, y = lax.axis_index("xlo"), lax.axis_index("y")
    me = lax.axis_index("xhi") * 2 + lax.axis_index("core")
    kp, qp = pack(queries, keys, values, tan_queries, tan_keys, tan_values)

    across = lax.ppermute(out_weight, ("xlo", "xhi"), [(2, 1), (1, 2), (3, 0), (0, 3)])

    r1, l1 = shift(kp, "z", 1), shift(kp, "z", -1)
    q0 = jnp.stack([qp, shift(qp, "xlo", 1)])
    qa, qb = shift(q0, "y", 1), shift(q0, "y", -1)
    r2, l2 = shift(r1, "z", 1), shift(l1, "z", -1)
    r2, l2, qa, qb = lax.optimization_barrier((r2, l2, qa, qb))
    qc = shift(q0, "y", 2)
    r3, l3 = shift(r2, "z", 1), shift(l2, "z", -1)
    qs = (q0, qa, qb, qc)
    at = jnp.stack([xlo, y]).astype(jnp.int32)

    state = attend(qs, (kp, r1, l1, r2, l2))
    r3, l3, *state = lax.optimization_barrier((r3, l3, *state))
    far = (shift(r3[: 2 * NH], "z", 1), shift(l3[2 * NH :], "z", -1))
    state = attend(qs, (r3, l3), state)
    sent = attend(qs, far, state, at)
    sent, across, out_weight = lax.optimization_barrier((sent, across, out_weight))
    weights = (out_weight, shift(out_weight, "core", 1), across, shift(across, "core", 1))
    got = lax.all_to_all(sent.reshape(32, PART, DH), ("xlo", "y", "xhi", "core"), 0, 0, tiled=True)
    return project(jnp.reshape(me, (1,)).astype(jnp.int32), got.reshape(8, 4, PART, DH), weights)


def solution(mesh):
    fine = Mesh(mesh.devices.reshape([SIZES[a] for a in AXES]), AXES)
    blk, head = ("xlo", "z", "y"), ("xhi", "core")
    spec = P(blk, head)
    return jax.shard_map(
        on_device,
        mesh=fine,
        in_specs=(spec,) * 6 + (P(head, None),),
        out_specs=(P(blk + head, None),) * 2,
        check_vma=False,
    )
```

```python
import functools
import math

import jax
import jax.numpy as jnp
from jax import lax
from jax.experimental import pallas as pl
from jax.experimental.pallas import tpu as pltpu
from jax.sharding import Mesh, PartitionSpec as P

DH = 128
NH = 3
TB = 128
SCALE = 1.0 / math.sqrt(DH)
SCALE2 = SCALE * math.log2(math.e)
SIZES = {"xlo": 2, "z": 8, "y": 4, "xhi": 2, "core": 2}
AXES = ("xlo", "z", "y", "xhi", "core")
PART = 2 * NH * 32 + 16
CHUNK = 512
F32, BF16 = jnp.float32, jnp.bfloat16
VMEM = pl.BlockSpec(memory_space=pltpu.VMEM)
SMEM = pl.BlockSpec(memory_space=pltpu.SMEM)


def shift(x, axis, by):
    n = SIZES[axis]
    return lax.ppermute(x, axis, [(i, (i + by) % n) for i in range(n)])


def mm(a, b):
    return jnp.dot(a, b, preferred_element_type=F32)


def pack_kernel(q, k, v, tq, tk, tv, kp, qp):
    for h in range(NH):
        cols = slice(h * DH, (h + 1) * DH)
        kp[2 * h] = k[:, cols]
        kp[2 * h + 1] = tk[:, cols]
        kp[2 * NH + 2 * h] = v[:, cols].T
        kp[2 * NH + 2 * h + 1] = tv[:, cols].T
        qp[2 * h] = q[:, cols].T
        qp[2 * h + 1] = tq[:, cols].T


def pack(q, k, v, tq, tk, tv):
    return pl.pallas_call(
        pack_kernel,
        out_shape=(
            jax.ShapeDtypeStruct((4 * NH, TB, DH), BF16),
            jax.ShapeDtypeStruct((2 * NH, DH, TB), BF16),
        ),
        in_specs=[VMEM] * 6,
        out_specs=(VMEM, VMEM),
        name="pack",
    )(q, k, v, tq, tk, tv)


def unit(qs, ks, vs, s, h):
    q = jnp.concatenate([qs[s][0, 2 * h], qs[s][1, 2 * h]], axis=1)
    tq = jnp.concatenate([qs[s][0, 2 * h + 1], qs[s][1, 2 * h + 1]], axis=1)
    k = jnp.concatenate([r[2 * h] for r in ks], axis=0)
    tk = jnp.concatenate([r[2 * h + 1] for r in ks], axis=0)
    scores = mm(k, q)
    tan = mm(jnp.concatenate([k, tk], axis=1), jnp.concatenate([tq, q], axis=0))
    return scores, tan


def attend_kernel(nk, first, last, *refs):
    refs = list(refs)
    at = refs.pop(0) if last else None
    qs = [refs.pop(0) for _ in range(4)]
    if nk == 0:
        kparts, vparts, vbase = [refs.pop(0)], [refs.pop(0)], 0
    else:
        kparts = [refs.pop(0) for _ in range(nk)]
        vparts, vbase = kparts, 2 * NH
    if not first:
        acc_in, st_in = refs.pop(0), refs.pop(0)
    if last:
        (out,) = refs
    else:
        acc_out, st_out = refs
    stat_rows = {}
    if last:
        places = [
            [lax.bitwise_xor(at[0], x) * 4 + lax.bitwise_and(at[1] + d, 3) for x in range(2)] for d in (0, 3, 1, 2)
        ]

    def finish(s, h, scores, tan):
        top = jnp.max(scores, axis=0, keepdims=True) * SCALE2
        if not first:
            st = st_in[s, h]
            old = st[0:1]
            top = jnp.maximum(old, top)
            keep = jnp.exp2(old - top)
        w = jnp.exp2(scores * SCALE2 - top)
        tw = w * tan
        den = jnp.sum(w, axis=0, keepdims=True)
        tden = jnp.sum(tw, axis=0, keepdims=True)
        wl, twl = w.astype(BF16), tw.astype(BF16)
        v = jnp.concatenate([r[vbase + 2 * h] for r in vparts], axis=1)
        tv = jnp.concatenate([r[vbase + 2 * h + 1] for r in vparts], axis=1)
        both = mm(jnp.concatenate([v, tv], axis=0), wl)
        a = both[:DH]
        b = both[DH:] + mm(v, twl) * SCALE
        if not first:
            a = a + acc_in[s, h, :DH] * keep
            b = b + acc_in[s, h, DH:] * keep
            den = den + st[1:2] * keep
            tden = tden + st[2:3] * keep
        if not last:
            acc_out[s, h, :DH] = a
            acc_out[s, h, DH:] = b
            st_out[s, h] = jnp.concatenate([top, den, tden, jnp.zeros((5, 2 * TB), F32)], axis=0)
            return
        inv = 1.0 / den
        ratio = tden * SCALE * inv
        o = a * inv
        t = b * inv - o * ratio
        lse = top + jnp.log2(den)
        l0 = lse.astype(BF16)
        rest = lse - l0.astype(F32)
        l1 = rest.astype(BF16)
        l2 = (rest - l1.astype(F32)).astype(BF16)
        r0 = ratio.astype(BF16)
        r1 = (ratio - r0.astype(F32)).astype(BF16)
        for x in range(2):
            lanes = slice(x * TB, (x + 1) * TB)
            ot = o[:, lanes].astype(BF16).T
            tt = t[:, lanes].astype(BF16).T
            for to in range(4):
                rows = slice(to * 32, (to + 1) * 32)
                out[places[s][x], to, 64 * h : 64 * h + 32] = ot[rows]
                out[places[s][x], to, 64 * h + 32 : 64 * h + 64] = tt[rows]
            stat_rows.setdefault((s, x), []).extend(
                piece[:, lanes].astype(F32) for piece in (l0, l1, l2, r0, r1)
            )
        if h == NH - 1:
            for x in range(2):
                rows = jnp.concatenate(stat_rows[s, x] + [jnp.zeros((1, TB), F32)], axis=0).astype(BF16)
                for to in range(4):
                    out[places[s][x], to, 64 * NH : PART] = rows

    waiting = []
    for s in range(4):
        for h in range(NH):
            waiting.append((s, h, *unit(qs, kparts, vparts, s, h)))
            if len(waiting) > 2:
                finish(*waiting.pop(0))
    for item in waiting:
        finish(*item)


def attend(qs, blocks, state=None, at=None):
    halves = blocks[0].shape[0] == 2 * NH
    first, last = state is None, at is not None
    nk = 0 if halves else len(blocks)
    keys = TB * max(nk, 1)
    operands = ([at] if last else []) + list(qs) + list(blocks) + ([] if first else list(state))
    specs = ([SMEM] if last else []) + [VMEM] * (len(operands) - last)
    if last:
        out_shape = jax.ShapeDtypeStruct((8, 4, PART, DH), BF16)
        out_specs = VMEM
    else:
        out_shape = (
            jax.ShapeDtypeStruct((4, NH, 2 * DH, 2 * TB), F32),
            jax.ShapeDtypeStruct((4, NH, 8, 2 * TB), F32),
        )
        out_specs = (VMEM, VMEM)
    n = len(operands)
    alias = {} if first or last else {n - 2: 0, n - 1: 1}
    return pl.pallas_call(
        functools.partial(attend_kernel, nk, first, last),
        out_shape=out_shape,
        in_specs=specs,
        out_specs=out_specs,
        input_output_aliases=alias,
        compiler_params=pltpu.CompilerParams(vmem_limit_bytes=16 << 20),
        cost_estimate=pl.CostEstimate(
            flops=2 * 8 * TB * DH * NH * keys * 8, bytes_accessed=8 << 20, transcendentals=8 * TB * NH * keys
        ),
        name=f"attend{keys}",
    )(*operands)


def project_kernel(me, got, w0, w1a, w1b, w2, w3a, w3b, out, tan_out, rows, w, total, sems):
    half = w1a.shape[0]
    whole = [
        [(w0, 0)],
        [(w1a, 0), (w1b, half)],
        [(w2, 0)],
        [(w3a, 0), (w3b, half)],
    ]
    copies = [
        [
            pltpu.make_async_copy(src, w.at[g, pl.ds(at, src.shape[0])], sems.at[g, i])
            for i, (src, at) in enumerate(parts)
        ]
        for g, parts in enumerate(whole)
    ]
    for copy in sum(copies, []):
        copy.start()
    share, tilt = [], []
    for g in range(4):
        st = got[:, lax.bitwise_xor(me[0], g), 64 * NH : PART].astype(F32)
        for h in range(NH):
            lse = st[:, 5 * h] + st[:, 5 * h + 1] + st[:, 5 * h + 2]
            ratio = st[:, 5 * h + 3] + st[:, 5 * h + 4]
            part_of = jnp.exp2(lse - jnp.max(lse, axis=0, keepdims=True))
            part_of = part_of / jnp.sum(part_of, axis=0, keepdims=True)
            share.append(part_of)
            tilt.append(part_of * (ratio - jnp.sum(part_of * ratio, axis=0, keepdims=True)))
    group = lax.broadcasted_iota(jnp.int32, (8, TB), 1) // 32
    part = lax.broadcasted_iota(jnp.int32, (8, TB), 0) % 4
    row = lax.broadcasted_iota(jnp.int32, (32, TB), 0)
    diagonal = lax.broadcasted_iota(jnp.int32, (32, TB), 1) % 32 == row

    def spread(w):
        turned = w
        for i in range(1, 4):
            turned = jnp.where(part == i, pltpu.roll(w, 32 * i, axis=1), turned)
        turned = pltpu.roll(turned, lax.rem(4 - me[0], 4) * 32, axis=1)
        picked = jnp.where(group == part, turned, 0.0)
        halves = [jnp.sum(picked[4 * i : 4 * i + 4], axis=0, keepdims=True) for i in range(2)]
        return jnp.concatenate([jnp.where(diagonal, half, 0.0) for half in halves], axis=1).astype(BF16)

    for g in range(4):
        j = lax.bitwise_xor(me[0], g)
        for h in range(NH):
            mix = jnp.concatenate([spread(share[g * NH + h]), spread(tilt[g * NH + h])], axis=0)
            o = jnp.concatenate([got[i, j, 64 * h : 64 * h + 32] for i in range(8)], axis=0)
            t = jnp.concatenate([got[i, j, 64 * h + 32 : 64 * h + 64] for i in range(8)], axis=0)
            both = mm(mix, jnp.concatenate([o, t], axis=1))
            rows[g, :32, h * DH : (h + 1) * DH] = both[:32, :DH].astype(BF16)
            rows[g, 32:, h * DH : (h + 1) * DH] = (both[:32, DH:] + both[32:, :DH]).astype(BF16)

    for g in range(4):
        for copy in copies[g]:
            copy.wait()
        for c in range(0, out.shape[1], CHUNK):
            cols = slice(c, c + CHUNK)
            term = mm(rows[g], w[g, :, cols])
            if g == 0:
                total[:, cols] = term
            elif g < 3:
                total[:, cols] += term
            else:
                term = term + total[:, cols]
                out[:, cols] = term[:32].astype(BF16)
                tan_out[:, cols] = term[32:].astype(BF16)


def project(me, got, weights):
    depth, width = weights[0].shape
    oshape = jax.ShapeDtypeStruct((32, width), BF16)
    return pl.pallas_call(
        project_kernel,
        out_shape=(oshape, oshape),
        in_specs=[SMEM, VMEM] + [pl.BlockSpec(memory_space=pl.ANY)] * 6,
        out_specs=(VMEM, VMEM),
        scratch_shapes=[
            pltpu.VMEM((4, 64, NH * DH), BF16),
            pltpu.VMEM((4, depth, width), BF16),
            pltpu.VMEM((64, width), F32),
            pltpu.SemaphoreType.DMA((4, 2)),
        ],
        compiler_params=pltpu.CompilerParams(vmem_limit_bytes=20 << 20),
        cost_estimate=pl.CostEstimate(
            flops=2 * 64 * 4 * depth * width, bytes_accessed=4 * depth * width * 2, transcendentals=0
        ),
        name="project",
    )(me, got, *weights)


def on_device(queries, keys, values, tan_queries, tan_keys, tan_values, out_weight):
    xlo, y = lax.axis_index("xlo"), lax.axis_index("y")
    me = lax.axis_index("xhi") * 2 + lax.axis_index("core")
    kp, qp = pack(queries, keys, values, tan_queries, tan_keys, tan_values)

    across = lax.ppermute(out_weight, ("xlo", "xhi"), [(2, 1), (1, 2), (3, 0), (0, 3)])

    r1, l1 = shift(kp, "z", 1), shift(kp, "z", -1)
    q0 = jnp.stack([qp, shift(qp, "xlo", 1)])
    qa, qb = shift(q0, "y", 1), shift(q0, "y", -1)
    r2, l2 = shift(r1, "z", 1), shift(l1, "z", -1)
    q0, qa, qb = lax.optimization_barrier((q0, qa, qb))
    qc = shift(q0, "y", 2)
    r3, l3 = shift(r2, "z", 1), shift(l2, "z", -1)
    qs = (q0, qa, qb, qc)
    at = jnp.stack([xlo, y]).astype(jnp.int32)

    state = attend(qs, (kp, r1, l1))
    r3, l3, *state = lax.optimization_barrier((r3, l3, *state))
    far = (shift(r3[: 2 * NH], "z", 1), shift(l3[2 * NH :], "z", -1))
    state = attend(qs, (r2, l2, r3, l3), state)
    sent = attend(qs, far, state, at)
    got = lax.all_to_all(sent.reshape(32, PART, DH), ("xlo", "y", "xhi", "core"), 0, 0, tiled=True)
    across, own = lax.optimization_barrier((across, out_weight))
    half = out_weight.shape[0] // 2
    other = [shift(own[i : i + half], "core", 1) for i in (0, half)]
    across_other = [shift(across[i : i + half], "core", 1) for i in (0, half)]
    weights = (out_weight, *other, across, *across_other)
    return project(jnp.reshape(me, (1,)).astype(jnp.int32), got.reshape(8, 4, PART, DH), weights)


def solution(mesh):
    fine = Mesh(mesh.devices.reshape([SIZES[a] for a in AXES]), AXES)
    blk, head = ("xlo", "z", "y"), ("xhi", "core")
    spec = P(blk, head)
    return jax.shard_map(
        on_device,
        mesh=fine,
        in_specs=(spec,) * 6 + (P(head, None),),
        out_specs=(P(blk + head, None),) * 2,
        check_vma=False,
    )
```

```python
import functools
import math

import jax
import jax.numpy as jnp
from jax import lax
from jax.experimental import pallas as pl
from jax.experimental.pallas import tpu as pltpu
from jax.sharding import Mesh, PartitionSpec as P

DH = 128
NH = 3
TB = 128
SCALE = 1.0 / math.sqrt(DH)
SCALE2 = SCALE * math.log2(math.e)
SIZES = {"xlo": 2, "z": 8, "y": 4, "xhi": 2, "core": 2}
AXES = ("xlo", "z", "y", "xhi", "core")
PART = 2 * NH * 32 + 16
CHUNK = 512
F32, BF16 = jnp.float32, jnp.bfloat16
VMEM = pl.BlockSpec(memory_space=pltpu.VMEM)
SMEM = pl.BlockSpec(memory_space=pltpu.SMEM)
HBM = pl.BlockSpec(memory_space=pltpu.HBM)


def shift(x, axis, by):
    n = SIZES[axis]
    return lax.ppermute(x, axis, [(i, (i + by) % n) for i in range(n)])


def mm(a, b):
    return jnp.dot(a, b, preferred_element_type=F32)


def pack_keys(k, v, tk, tv, kp):
    for h in range(NH):
        cols = slice(h * DH, (h + 1) * DH)
        kp[2 * h] = k[:, cols]
        kp[2 * h + 1] = tk[:, cols]
        kp[2 * NH + 2 * h] = v[:, cols].T
        kp[2 * NH + 2 * h + 1] = tv[:, cols].T


def pack_kernel(q, k, v, tq, tk, tv, kp, qp):
    pack_keys(k, v, tk, tv, kp)
    for h in range(NH):
        cols = slice(h * DH, (h + 1) * DH)
        qp[2 * h] = q[:, cols].T
        qp[2 * h + 1] = tq[:, cols].T


def pack(q, k, v, tq, tk, tv):
    return pl.pallas_call(
        pack_kernel,
        out_shape=(
            jax.ShapeDtypeStruct((4 * NH, TB, DH), BF16),
            jax.ShapeDtypeStruct((2 * NH, DH, TB), BF16),
        ),
        in_specs=[VMEM] * 6,
        out_specs=(VMEM, VMEM),
        name="pack",
    )(q, k, v, tq, tk, tv)


def scores_of(q_ref, kparts, h):
    q = jnp.concatenate([q_ref[0, 2 * h], q_ref[1, 2 * h]], axis=1)
    tq = jnp.concatenate([q_ref[0, 2 * h + 1], q_ref[1, 2 * h + 1]], axis=1)
    k = jnp.concatenate([r[2 * h] for r in kparts], axis=0)
    tk = jnp.concatenate([r[2 * h + 1] for r in kparts], axis=0)
    return mm(k, q), mm(jnp.concatenate([k, tk], axis=1), jnp.concatenate([tq, q], axis=0))


def absorb(scores, tan, vparts, vbase, h, state):
    top = jnp.max(scores, axis=0, keepdims=True) * SCALE2
    if state is not None:
        acc, st = state
        top = jnp.maximum(st[0:1], top)
        keep = jnp.exp2(st[0:1] - top)
    w = jnp.exp2(scores * SCALE2 - top)
    tw = w * tan
    den = jnp.sum(w, axis=0, keepdims=True)
    tden = jnp.sum(tw, axis=0, keepdims=True)
    v = jnp.concatenate([r[vbase + 2 * h] for r in vparts], axis=1)
    tv = jnp.concatenate([r[vbase + 2 * h + 1] for r in vparts], axis=1)
    both = mm(jnp.concatenate([v, tv], axis=0), w.astype(BF16))
    a = both[:DH]
    b = both[DH:] + mm(v, tw.astype(BF16)) * SCALE
    if state is not None:
        a = a + acc[:DH] * keep
        b = b + acc[DH:] * keep
        den = den + st[1:2] * keep
        tden = tden + st[2:3] * keep
    return top, den, tden, a, b


def pipeline(units):
    waiting = []
    for front, back in units:
        waiting.append((back, front()))
        if len(waiting) > 2:
            ready, made = waiting.pop(0)
            ready(*made)
    for ready, made in waiting:
        ready(*made)


def attend_kernel(plan, nk, had, *refs):
    qs, blocks, refs = refs[:4], refs[4 : 4 + nk], refs[4 + nk :]
    if had:
        acc_in, st_in, acc_out, st_out = refs
    else:
        acc_out, st_out, own = refs
        pack_keys(*blocks[:4], own)
        blocks = (own, *blocks[4:])

    def make(s, h):
        parts = [blocks[i] for i in plan[s][0]]

        def back(scores, tan):
            state = (acc_in[s, h], st_in[s, h]) if plan[s][1] else None
            top, den, tden, a, b = absorb(scores, tan, parts, 2 * NH, h, state)
            acc_out[s, h, :DH] = a
            acc_out[s, h, DH:] = b
            st_out[s, h] = jnp.concatenate([top, den, tden, jnp.zeros((5, 2 * TB), F32)], axis=0)

        return lambda: scores_of(qs[s], parts, h), back

    pipeline([make(s, h) for s in range(4) for h in range(NH) if plan[s][0]])


def attend(qs, blocks, plan, state=()):
    operands = [*qs, *blocks, *state]
    n, had = len(operands), bool(state)
    keys = TB * sum(len(numbers) for numbers, _ in plan)
    return pl.pallas_call(
        functools.partial(attend_kernel, plan, len(blocks), had),
        out_shape=(
            jax.ShapeDtypeStruct((4, NH, 2 * DH, 2 * TB), F32),
            jax.ShapeDtypeStruct((4, NH, 8, 2 * TB), F32),
        ),
        in_specs=[VMEM] * n,
        out_specs=(VMEM, VMEM),
        input_output_aliases={n - 2: 0, n - 1: 1} if had else {},
        scratch_shapes=[] if had else [pltpu.VMEM((4 * NH, TB, DH), BF16)],
        compiler_params=pltpu.CompilerParams(vmem_limit_bytes=16 << 20),
        cost_estimate=pl.CostEstimate(
            flops=2 * 2 * TB * DH * NH * keys * 8, bytes_accessed=8 << 20, transcendentals=2 * TB * NH * keys
        ),
        name=f"attend{keys}",
    )(*operands)


def close_kernel(at, q0, q1, q2, q3, kfar, vfar, acc, st, out, held, sems):
    qs = (q0, q1, q2, q3)
    places = [[lax.bitwise_xor(at[0], x) * 4 + lax.bitwise_and(at[1] + d, 3) for x in range(2)] for d in (0, 3, 1, 2)]
    stat_rows, copies = {}, []

    def make(s, h):
        def back(scores, tan):
            top, den, tden, a, b = absorb(scores, tan, [vfar], 0, h, (acc[s, h], st[s, h]))
            inv = 1.0 / den
            ratio = tden * SCALE * inv
            o = a * inv
            t = b * inv - o * ratio
            lse = top + jnp.log2(den)
            l0 = lse.astype(BF16)
            rest = lse - l0.astype(F32)
            l1 = rest.astype(BF16)
            l2 = (rest - l1.astype(F32)).astype(BF16)
            r0 = ratio.astype(BF16)
            r1 = (ratio - r0.astype(F32)).astype(BF16)
            for x in range(2):
                lanes = slice(x * TB, (x + 1) * TB)
                ot, tt = o[:, lanes].astype(BF16).T, t[:, lanes].astype(BF16).T
                for to in range(4):
                    rows = slice(to * 32, (to + 1) * 32)
                    held[2 * s + x, to, 64 * h : 64 * h + 32] = ot[rows]
                    held[2 * s + x, to, 64 * h + 32 : 64 * h + 64] = tt[rows]
                stat_rows.setdefault((s, x), []).extend(
                    piece[:, lanes].astype(F32) for piece in (l0, l1, l2, r0, r1)
                )
            if h == NH - 1:
                for x in range(2):
                    rows = jnp.concatenate(stat_rows[s, x] + [jnp.zeros((1, TB), F32)], axis=0).astype(BF16)
                    for to in range(4):
                        held[2 * s + x, to, 64 * NH : PART] = rows
                    copies.append(
                        pltpu.make_async_copy(held.at[2 * s + x], out.at[places[s][x]], sems.at[2 * s + x])
                    )
                    copies[-1].start()

        return lambda: scores_of(qs[s], [kfar], h), back

    pipeline([make(s, h) for s in range(4) for h in range(NH)])
    for copy in copies:
        copy.wait()


def close(at, qs, far, state):
    return pl.pallas_call(
        close_kernel,
        out_shape=jax.ShapeDtypeStruct((8, 4, PART, DH), BF16),
        in_specs=[SMEM] + [VMEM] * 8,
        out_specs=HBM,
        scratch_shapes=[pltpu.VMEM((8, 4, PART, DH), BF16), pltpu.SemaphoreType.DMA((8,))],
        compiler_params=pltpu.CompilerParams(vmem_limit_bytes=16 << 20),
        cost_estimate=pl.CostEstimate(
            flops=2 * 8 * TB * DH * NH * TB * 8, bytes_accessed=8 << 20, transcendentals=8 * TB * NH * TB
        ),
        name="close",
    )(at, *qs, *far, *state)


def project_kernel(me, got_hbm, w0, w1a, w1b, w2, w3a, w3b, out, tan_out, rows, w, total, got, sems, got_sem):
    received = pltpu.make_async_copy(got_hbm, got, got_sem)
    received.start()
    half = w1a.shape[0]
    whole = [
        [(w0, 0)],
        [(w1a, 0), (w1b, half)],
        [(w2, 0)],
        [(w3a, 0), (w3b, half)],
    ]
    copies = [
        [
            pltpu.make_async_copy(src, w.at[g, pl.ds(at, src.shape[0])], sems.at[g, i])
            for i, (src, at) in enumerate(parts)
        ]
        for g, parts in enumerate(whole)
    ]
    for copy in sum(copies, []):
        copy.start()
    received.wait()
    share, tilt = [], []
    for g in range(4):
        st = got[:, lax.bitwise_xor(me[0], g), 64 * NH : PART].astype(F32)
        for h in range(NH):
            lse = st[:, 5 * h] + st[:, 5 * h + 1] + st[:, 5 * h + 2]
            ratio = st[:, 5 * h + 3] + st[:, 5 * h + 4]
            part_of = jnp.exp2(lse - jnp.max(lse, axis=0, keepdims=True))
            part_of = part_of / jnp.sum(part_of, axis=0, keepdims=True)
            share.append(part_of)
            tilt.append(part_of * (ratio - jnp.sum(part_of * ratio, axis=0, keepdims=True)))
    group = lax.broadcasted_iota(jnp.int32, (8, TB), 1) // 32
    part = lax.broadcasted_iota(jnp.int32, (8, TB), 0) % 4
    row = lax.broadcasted_iota(jnp.int32, (32, TB), 0)
    diagonal = lax.broadcasted_iota(jnp.int32, (32, TB), 1) % 32 == row

    def spread(w):
        turned = w
        for i in range(1, 4):
            turned = jnp.where(part == i, pltpu.roll(w, 32 * i, axis=1), turned)
        turned = pltpu.roll(turned, lax.rem(4 - me[0], 4) * 32, axis=1)
        picked = jnp.where(group == part, turned, 0.0)
        halves = [jnp.sum(picked[4 * i : 4 * i + 4], axis=0, keepdims=True) for i in range(2)]
        return jnp.concatenate([jnp.where(diagonal, half, 0.0) for half in halves], axis=1).astype(BF16)

    for g in range(4):
        j = lax.bitwise_xor(me[0], g)
        for h in range(NH):
            mix = jnp.concatenate([spread(share[g * NH + h]), spread(tilt[g * NH + h])], axis=0)
            o = jnp.concatenate([got[i, j, 64 * h : 64 * h + 32] for i in range(8)], axis=0)
            t = jnp.concatenate([got[i, j, 64 * h + 32 : 64 * h + 64] for i in range(8)], axis=0)
            both = mm(mix, jnp.concatenate([o, t], axis=1))
            rows[g, :32, h * DH : (h + 1) * DH] = both[:32, :DH].astype(BF16)
            rows[g, 32:, h * DH : (h + 1) * DH] = (both[:32, DH:] + both[32:, :DH]).astype(BF16)

    for g in range(4):
        for copy in copies[g]:
            copy.wait()
        for c in range(0, out.shape[1], CHUNK):
            cols = slice(c, c + CHUNK)
            term = mm(rows[g], w[g, :, cols])
            if g == 0:
                total[:, cols] = term
            elif g < 3:
                total[:, cols] += term
            else:
                term = term + total[:, cols]
                out[:, cols] = term[:32].astype(BF16)
                tan_out[:, cols] = term[32:].astype(BF16)


def project(me, got, weights):
    depth, width = weights[0].shape
    oshape = jax.ShapeDtypeStruct((32, width), BF16)
    return pl.pallas_call(
        project_kernel,
        out_shape=(oshape, oshape),
        in_specs=[SMEM] + [pl.BlockSpec(memory_space=pl.ANY)] * 7,
        out_specs=(VMEM, VMEM),
        scratch_shapes=[
            pltpu.VMEM((4, 64, NH * DH), BF16),
            pltpu.VMEM((4, depth, width), BF16),
            pltpu.VMEM((64, width), F32),
            pltpu.VMEM((8, 4, PART, DH), BF16),
            pltpu.SemaphoreType.DMA((4, 2)),
            pltpu.SemaphoreType.DMA,
        ],
        compiler_params=pltpu.CompilerParams(vmem_limit_bytes=20 << 20),
        cost_estimate=pl.CostEstimate(
            flops=2 * 64 * 4 * depth * width, bytes_accessed=4 * depth * width * 2, transcendentals=0
        ),
        name="project",
    )(me, got, *weights)


def on_device(queries, keys, values, tan_queries, tan_keys, tan_values, out_weight):
    xlo, y = lax.axis_index("xlo"), lax.axis_index("y")
    me = lax.axis_index("xhi") * 2 + lax.axis_index("core")
    kp, qp = pack(queries, keys, values, tan_queries, tan_keys, tan_values)

    across = lax.ppermute(out_weight, ("xlo", "xhi"), [(2, 1), (1, 2), (3, 0), (0, 3)])

    r1, l1 = shift(kp, "z", 1), shift(kp, "z", -1)
    q0 = jnp.stack([qp, shift(qp, "xlo", 1)])
    qa, qb = shift(q0, "y", 1), shift(q0, "y", -1)
    r2, l2 = shift(r1, "z", 1), shift(l1, "z", -1)
    q0, qa, qb = lax.optimization_barrier((q0, qa, qb))
    qc = shift(q0, "y", 2)
    r3, l3 = shift(r2, "z", 1), shift(l2, "z", -1)
    qs = (q0, qa, qb, qc)
    at = jnp.stack([xlo, y]).astype(jnp.int32)

    state = attend(qs, (keys, values, tan_keys, tan_values, r1, l1, r2), [((0, 1, 2, 3), False)] * 4)
    r3, l3, *state = lax.optimization_barrier((r3, l3, *state))
    far = (shift(r3[: 2 * NH], "z", 1), shift(l3[2 * NH :], "z", -1))
    state = attend(qs, (l2, r3, l3), [((0, 1, 2), True)] * 4, state)
    sent = close(at, qs, far, state)
    got = lax.all_to_all(sent.reshape(32, PART, DH), ("xlo", "y", "xhi", "core"), 0, 0, tiled=True)
    across, own = lax.optimization_barrier((across, out_weight))
    half = out_weight.shape[0] // 2
    other = [shift(own[i : i + half], "core", 1) for i in (0, half)]
    across_other = [shift(across[i : i + half], "core", 1) for i in (0, half)]
    weights = (out_weight, *other, across, *across_other)
    return project(jnp.reshape(me, (1,)).astype(jnp.int32), got.reshape(8, 4, PART, DH), weights)


def solution(mesh):
    fine = Mesh(mesh.devices.reshape([SIZES[a] for a in AXES]), AXES)
    blk, head = ("xlo", "z", "y"), ("xhi", "core")
    spec = P(blk, head)
    return jax.shard_map(
        on_device,
        mesh=fine,
        in_specs=(spec,) * 6 + (P(head, None),),
        out_specs=(P(blk + head, None),) * 2,
        check_vma=False,
    )
```

```python
import functools
import math

import jax
import jax.numpy as jnp
from jax import lax
from jax.experimental import pallas as pl
from jax.experimental.pallas import tpu as pltpu
from jax.sharding import Mesh, PartitionSpec as P

DH = 128
NH = 3
TB = 128
SCALE = 1.0 / math.sqrt(DH)
SCALE2 = SCALE * math.log2(math.e)
SIZES = {"xlo": 2, "z": 8, "y": 4, "xhi": 2, "core": 2}
AXES = ("xlo", "z", "y", "xhi", "core")
PART = 2 * NH * 32 + 16
CHUNK = 512
F32, BF16 = jnp.float32, jnp.bfloat16
VMEM = pl.BlockSpec(memory_space=pltpu.VMEM)
SMEM = pl.BlockSpec(memory_space=pltpu.SMEM)
HBM = pl.BlockSpec(memory_space=pltpu.HBM)


def shift(x, axis, by):
    n = SIZES[axis]
    return lax.ppermute(x, axis, [(i, (i + by) % n) for i in range(n)])


def mm(a, b):
    return jnp.dot(a, b, preferred_element_type=F32)


def pack_keys(k, v, tk, tv, kp):
    for h in range(NH):
        cols = slice(h * DH, (h + 1) * DH)
        kp[2 * h] = k[:, cols]
        kp[2 * h + 1] = tk[:, cols]
        kp[2 * NH + 2 * h] = v[:, cols].T
        kp[2 * NH + 2 * h + 1] = tv[:, cols].T


def pack_kernel(q, k, v, tq, tk, tv, kp, qp):
    pack_keys(k, v, tk, tv, kp)
    for h in range(NH):
        cols = slice(h * DH, (h + 1) * DH)
        qp[2 * h] = q[:, cols].T
        qp[2 * h + 1] = tq[:, cols].T


def pack(q, k, v, tq, tk, tv):
    return pl.pallas_call(
        pack_kernel,
        out_shape=(
            jax.ShapeDtypeStruct((4 * NH, TB, DH), BF16),
            jax.ShapeDtypeStruct((2 * NH, DH, TB), BF16),
        ),
        in_specs=[VMEM] * 6,
        out_specs=(VMEM, VMEM),
        name="pack",
    )(q, k, v, tq, tk, tv)


def scores_of(q_ref, kparts, h):
    q = jnp.concatenate([q_ref[0, 2 * h], q_ref[1, 2 * h]], axis=1)
    tq = jnp.concatenate([q_ref[0, 2 * h + 1], q_ref[1, 2 * h + 1]], axis=1)
    k = jnp.concatenate([r[2 * h] for r in kparts], axis=0)
    tk = jnp.concatenate([r[2 * h + 1] for r in kparts], axis=0)
    return mm(k, q), mm(jnp.concatenate([k, tk], axis=1), jnp.concatenate([tq, q], axis=0))


def absorb(scores, tan, vparts, vbase, h, state):
    top = jnp.max(scores, axis=0, keepdims=True) * SCALE2
    if state is not None:
        acc, st = state
        top = jnp.maximum(st[0:1], top)
        keep = jnp.exp2(st[0:1] - top)
    w = jnp.exp2(scores * SCALE2 - top)
    tw = w * tan
    den = jnp.sum(w, axis=0, keepdims=True)
    tden = jnp.sum(tw, axis=0, keepdims=True)
    v = jnp.concatenate([r[vbase + 2 * h] for r in vparts], axis=1)
    tv = jnp.concatenate([r[vbase + 2 * h + 1] for r in vparts], axis=1)
    both = mm(jnp.concatenate([v, tv], axis=0), w.astype(BF16))
    a = both[:DH]
    b = both[DH:] + mm(v, tw.astype(BF16)) * SCALE
    if state is not None:
        a = a + acc[:DH] * keep
        b = b + acc[DH:] * keep
        den = den + st[1:2] * keep
        tden = tden + st[2:3] * keep
    return top, den, tden, a, b


def pipeline(units):
    waiting = []
    for front, back in units:
        waiting.append((back, front()))
        if len(waiting) > 2:
            ready, made = waiting.pop(0)
            ready(*made)
    for ready, made in waiting:
        ready(*made)


def attend_kernel(plan, nk, had, *refs):
    qs, blocks, refs = refs[:4], refs[4 : 4 + nk], refs[4 + nk :]
    if had:
        acc_in, st_in, acc_out, st_out = refs
    else:
        acc_out, st_out, own = refs
        pack_keys(*blocks[:4], own)
        blocks = (own, *blocks[4:])

    def make(s, h):
        parts = [blocks[i] for i in plan[s][0]]

        def back(scores, tan):
            state = (acc_in[s, h], st_in[s, h]) if plan[s][1] else None
            top, den, tden, a, b = absorb(scores, tan, parts, 2 * NH, h, state)
            acc_out[s, h, :DH] = a
            acc_out[s, h, DH:] = b
            st_out[s, h] = jnp.concatenate([top, den, tden, jnp.zeros((5, 2 * TB), F32)], axis=0)

        return lambda: scores_of(qs[s], parts, h), back

    pipeline([make(s, h) for s in range(4) for h in range(NH) if plan[s][0]])


def attend(qs, blocks, plan, state=()):
    operands = [*qs, *blocks, *state]
    n, had = len(operands), bool(state)
    keys = TB * sum(len(numbers) for numbers, _ in plan)
    return pl.pallas_call(
        functools.partial(attend_kernel, plan, len(blocks), had),
        out_shape=(
            jax.ShapeDtypeStruct((4, NH, 2 * DH, 2 * TB), F32),
            jax.ShapeDtypeStruct((4, NH, 8, 2 * TB), F32),
        ),
        in_specs=[VMEM] * n,
        out_specs=(VMEM, VMEM),
        input_output_aliases={n - 2: 0, n - 1: 1} if had else {},
        scratch_shapes=[] if had else [pltpu.VMEM((4 * NH, TB, DH), BF16)],
        compiler_params=pltpu.CompilerParams(vmem_limit_bytes=16 << 20),
        cost_estimate=pl.CostEstimate(
            flops=2 * 2 * TB * DH * NH * keys * 8, bytes_accessed=8 << 20, transcendentals=2 * TB * NH * keys
        ),
        name=f"attend{keys}",
    )(*operands)


def close_kernel(at, q0, q1, q2, q3, kfar, vfar, acc, st, out, held, sems):
    qs = (q0, q1, q2, q3)
    places = [[lax.bitwise_xor(at[0], x) * 4 + lax.bitwise_and(at[1] + d, 3) for x in range(2)] for d in (0, 3, 1, 2)]
    stat_rows, copies = {}, []

    def make(s, h):
        def back(scores, tan):
            top, den, tden, a, b = absorb(scores, tan, [vfar], 0, h, (acc[s, h], st[s, h]))
            inv = 1.0 / den
            ratio = tden * SCALE * inv
            o = a * inv
            t = b * inv - o * ratio
            lse = top + jnp.log2(den)
            l0 = lse.astype(BF16)
            rest = lse - l0.astype(F32)
            l1 = rest.astype(BF16)
            l2 = (rest - l1.astype(F32)).astype(BF16)
            r0 = ratio.astype(BF16)
            r1 = (ratio - r0.astype(F32)).astype(BF16)
            for x in range(2):
                lanes = slice(x * TB, (x + 1) * TB)
                ot, tt = o[:, lanes].astype(BF16).T, t[:, lanes].astype(BF16).T
                for to in range(4):
                    rows = slice(to * 32, (to + 1) * 32)
                    held[2 * s + x, to, 64 * h : 64 * h + 32] = ot[rows]
                    held[2 * s + x, to, 64 * h + 32 : 64 * h + 64] = tt[rows]
                stat_rows.setdefault((s, x), []).extend(
                    piece[:, lanes].astype(F32) for piece in (l0, l1, l2, r0, r1)
                )
            if h == NH - 1:
                for x in range(2):
                    rows = jnp.concatenate(stat_rows[s, x] + [jnp.zeros((1, TB), F32)], axis=0).astype(BF16)
                    for to in range(4):
                        held[2 * s + x, to, 64 * NH : PART] = rows
                    copies.append(
                        pltpu.make_async_copy(held.at[2 * s + x], out.at[places[s][x]], sems.at[2 * s + x])
                    )
                    copies[-1].start()

        return lambda: scores_of(qs[s], [kfar], h), back

    pipeline([make(s, h) for s in range(4) for h in range(NH)])
    for copy in copies:
        copy.wait()


def close(at, qs, far, state):
    return pl.pallas_call(
        close_kernel,
        out_shape=jax.ShapeDtypeStruct((8, 4, PART, DH), BF16),
        in_specs=[SMEM] + [VMEM] * 8,
        out_specs=HBM,
        scratch_shapes=[pltpu.VMEM((8, 4, PART, DH), BF16), pltpu.SemaphoreType.DMA((8,))],
        compiler_params=pltpu.CompilerParams(vmem_limit_bytes=16 << 20),
        cost_estimate=pl.CostEstimate(
            flops=2 * 8 * TB * DH * NH * TB * 8, bytes_accessed=8 << 20, transcendentals=8 * TB * NH * TB
        ),
        name="close",
    )(at, *qs, *far, *state)


def project_kernel(me, got_hbm, w0, w1a, w1b, w2, w3a, w3b, out, tan_out, rows, w, total, got, sems, got_sem):
    received = pltpu.make_async_copy(got_hbm, got, got_sem)
    received.start()
    half = w1a.shape[0]
    whole = [
        [(w0, 0)],
        [(w1a, 0), (w1b, half)],
        [(w2, 0)],
        [(w3a, 0), (w3b, half)],
    ]
    copies = [
        [
            pltpu.make_async_copy(src, w.at[g, pl.ds(at, src.shape[0])], sems.at[g, i])
            for i, (src, at) in enumerate(parts)
        ]
        for g, parts in enumerate(whole)
    ]
    for copy in sum(copies, []):
        copy.start()
    received.wait()
    share, tilt = [], []
    for g in range(4):
        st = got[:, lax.bitwise_xor(me[0], g), 64 * NH : PART].astype(F32)
        for h in range(NH):
            lse = st[:, 5 * h] + st[:, 5 * h + 1] + st[:, 5 * h + 2]
            ratio = st[:, 5 * h + 3] + st[:, 5 * h + 4]
            part_of = jnp.exp2(lse - jnp.max(lse, axis=0, keepdims=True))
            part_of = part_of / jnp.sum(part_of, axis=0, keepdims=True)
            share.append(part_of)
            tilt.append(part_of * (ratio - jnp.sum(part_of * ratio, axis=0, keepdims=True)))
    group = lax.broadcasted_iota(jnp.int32, (8, TB), 1) // 32
    part = lax.broadcasted_iota(jnp.int32, (8, TB), 0) % 4
    row = lax.broadcasted_iota(jnp.int32, (32, TB), 0)
    diagonal = lax.broadcasted_iota(jnp.int32, (32, TB), 1) % 32 == row

    def spread(w):
        turned = w
        for i in range(1, 4):
            turned = jnp.where(part == i, pltpu.roll(w, 32 * i, axis=1), turned)
        turned = pltpu.roll(turned, lax.rem(4 - me[0], 4) * 32, axis=1)
        picked = jnp.where(group == part, turned, 0.0)
        halves = [jnp.sum(picked[4 * i : 4 * i + 4], axis=0, keepdims=True) for i in range(2)]
        return jnp.concatenate([jnp.where(diagonal, half, 0.0) for half in halves], axis=1).astype(BF16)

    for g in range(4):
        j = lax.bitwise_xor(me[0], g)
        for h in range(NH):
            mix = jnp.concatenate([spread(share[g * NH + h]), spread(tilt[g * NH + h])], axis=0)
            o = jnp.concatenate([got[i, j, 64 * h : 64 * h + 32] for i in range(8)], axis=0)
            t = jnp.concatenate([got[i, j, 64 * h + 32 : 64 * h + 64] for i in range(8)], axis=0)
            both = mm(mix, jnp.concatenate([o, t], axis=1))
            rows[g, :32, h * DH : (h + 1) * DH] = both[:32, :DH].astype(BF16)
            rows[g, 32:, h * DH : (h + 1) * DH] = (both[:32, DH:] + both[32:, :DH]).astype(BF16)

    for g in range(4):
        for copy in copies[g]:
            copy.wait()
        for c in range(0, out.shape[1], CHUNK):
            cols = slice(c, c + CHUNK)
            term = mm(rows[g], w[g, :, cols])
            if g == 0:
                total[:, cols] = term
            elif g < 3:
                total[:, cols] += term
            else:
                term = term + total[:, cols]
                out[:, cols] = term[:32].astype(BF16)
                tan_out[:, cols] = term[32:].astype(BF16)


def project(me, got, weights):
    depth, width = weights[0].shape
    oshape = jax.ShapeDtypeStruct((32, width), BF16)
    return pl.pallas_call(
        project_kernel,
        out_shape=(oshape, oshape),
        in_specs=[SMEM] + [pl.BlockSpec(memory_space=pl.ANY)] * 7,
        out_specs=(VMEM, VMEM),
        scratch_shapes=[
            pltpu.VMEM((4, 64, NH * DH), BF16),
            pltpu.VMEM((4, depth, width), BF16),
            pltpu.VMEM((64, width), F32),
            pltpu.VMEM((8, 4, PART, DH), BF16),
            pltpu.SemaphoreType.DMA((4, 2)),
            pltpu.SemaphoreType.DMA,
        ],
        compiler_params=pltpu.CompilerParams(vmem_limit_bytes=20 << 20),
        cost_estimate=pl.CostEstimate(
            flops=2 * 64 * 4 * depth * width, bytes_accessed=4 * depth * width * 2, transcendentals=0
        ),
        name="project",
    )(me, got, *weights)


def on_device(queries, keys, values, tan_queries, tan_keys, tan_values, out_weight):
    xlo, y = lax.axis_index("xlo"), lax.axis_index("y")
    me = lax.axis_index("xhi") * 2 + lax.axis_index("core")
    kp, qp = pack(queries, keys, values, tan_queries, tan_keys, tan_values)

    _, qp = lax.optimization_barrier((shift(kp[0, :16], "core", 1), qp))
    across = lax.ppermute(out_weight, ("xlo", "xhi"), [(2, 1), (1, 2), (3, 0), (0, 3)])

    r1, l1 = shift(kp, "z", 1), shift(kp, "z", -1)
    q0 = jnp.stack([qp, shift(qp, "xlo", 1)])
    qa, qb = shift(q0, "y", 1), shift(q0, "y", -1)
    r2, l2 = shift(r1, "z", 1), shift(l1, "z", -1)
    q0, qa, qb = lax.optimization_barrier((q0, qa, qb))
    qc = shift(q0, "y", 2)
    r3, l3 = shift(r2, "z", 1), shift(l2, "z", -1)
    qs = (q0, qa, qb, qc)
    at = jnp.stack([xlo, y]).astype(jnp.int32)

    state = attend(qs, (keys, values, tan_keys, tan_values, r1, l1, r2), [((0, 1, 2, 3), False)] * 4)
    r3, l3, *state = lax.optimization_barrier((r3, l3, *state))
    far = (shift(r3[: 2 * NH], "z", 1), shift(l3[2 * NH :], "z", -1))
    state = attend(qs, (l2, r3, l3), [((0, 1, 2), True)] * 4, state)
    sent = close(at, qs, far, state)
    got = lax.all_to_all(sent.reshape(32, PART, DH), ("xlo", "y", "xhi", "core"), 0, 0, tiled=True)
    across, own = lax.optimization_barrier((across, out_weight))
    half = out_weight.shape[0] // 2
    other = [shift(own[i : i + half], "core", 1) for i in (0, half)]
    across_other = [shift(across[i : i + half], "core", 1) for i in (0, half)]
    weights = (out_weight, *other, across, *across_other)
    return project(jnp.reshape(me, (1,)).astype(jnp.int32), got.reshape(8, 4, PART, DH), weights)


def solution(mesh):
    fine = Mesh(mesh.devices.reshape([SIZES[a] for a in AXES]), AXES)
    blk, head = ("xlo", "z", "y"), ("xhi", "core")
    spec = P(blk, head)
    return jax.shard_map(
        on_device,
        mesh=fine,
        in_specs=(spec,) * 6 + (P(head, None),),
        out_specs=(P(blk + head, None),) * 2,
        check_vma=False,
    )
```
